32 devices in a mesh: groups: 2 (over x), head: 16 (over z, y, core).
Axes of the slice: x: 2, y: 2, z: 4, core: 2. Of those that a mesh axis runs over, the one named last changes fastest.
Arguments:
- queries: bfloat16 [256, 2048], P('groups', 'head'), parts along dimension 0, may hold values from -400 to 400
- cache: bfloat16 [2, 8192, 128], P(None, ('groups', 'head')), parts along dimension 1, may hold values from -5 to 5
- cache_scale: bfloat16 [2, 1, 8192], P(None, None, ('groups', 'head')), parts along dimension 2, may hold values from 0.5 to 4
- offsets: int32 [4], P('groups'), parts along dimension 0, may hold values from 0 to 2048, as said below
- lengths: int32 [4], P('groups'), parts along dimension 0, may hold values from 64 to 2048, as said below
- clamp_code: int32 [2], P('groups'), parts along dimension 0, may hold values from 512 to 1535
- w_out: bfloat16 [2048, 16384], P('head'), may hold values from -0.125 to 0.125
Outputs:
- projected: bfloat16 [16384, 256], P('head', 'groups'), parts along dimension 1
The draws below stay inside these ranges and needn't reach their ends.
There are 2 independent parts, one for each index of `groups`. The reference program is written for one: setup_inputs(seed, part) draws one part's arguments, and reference() takes and returns one part's arrays. A program takes and returns all parts, laid end to end along the dimension named above; an argument that names none is the same for every part. Nothing has to cross between parts.
Inputs may be any that keep to these rules, and one draw needn't show every extreme that they name: Request r's cache region is offsets[r] to offsets[r] + lengths[r] - 1 and lies within positions r * 2048 to (r + 1) * 2048 - 1. `lengths`: the last 64 positions of each region hold the span's own keys and values; in every draw some request's length is exactly 2048.
All inputs are finite; a program needn't handle non-finite values.
Results may differ from the reference program's by a relative error of at most 0.0068.
Values may be sent and summed in bfloat16 or wider, within the bound.
A program may use at most 128 MiB of HBM per device.

```python
import math
import jax
import jax.numpy as jnp
from jax import lax

HD = 128
D = 16384
HEADS = 16
KVH = 1
REQS = 2
SPAN = 64
LEN = 4096
SEG = 2048


def layout(key):
    base_key = jax.random.fold_in(key, 7101)
    key_len, key_full, key_start = jax.random.split(base_key, 3)
    lengths = jax.random.randint(key_len, (REQS,), SPAN, SEG + 1)
    full_req = jax.random.randint(key_full, (), 0, REQS)
    req_index = jnp.arange(REQS, dtype=jnp.int32)
    lengths = jnp.where(req_index == full_req, SEG, lengths).astype(jnp.int32)
    start_shift = jax.random.randint(key_start, (REQS,), 0, 1 << 30) % (SEG - lengths + 1)
    start_shift = jnp.where(req_index == REQS - 1, 0, start_shift)
    offsets = (req_index * SEG + start_shift).astype(jnp.int32)
    return (offsets, lengths)


def cache_fields(key):
    base_key = jax.random.fold_in(key, 7202)
    key_keys, key_vals, key_mean, key_scale, key_query = jax.random.split(base_key, 5)
    keys_all = jax.random.truncated_normal(key_keys, -4.0, 4.0, (LEN, KVH * HD), jnp.float32)
    channel_mean = jax.random.uniform(key_mean, (1, KVH * HD), jnp.float32, -1.0, 1.0)
    values_all = jax.random.truncated_normal(key_vals, -4.0, 4.0, (LEN, KVH * HD), jnp.float32) + channel_mean
    scales = jnp.exp(jax.random.uniform(key_scale, (2, KVH, LEN), jnp.float32, math.log(0.5), math.log(4.0)))
    queries_all = jax.random.truncated_normal(key_query, -4.0, 4.0, (REQS * SPAN, HEADS * HD), jnp.float32)
    return (keys_all, values_all, scales, queries_all)


def draw_queries(key, part):
    return cache_fields(key)[3].astype(jnp.bfloat16)


def draw_cache(key, part):
    fields = cache_fields(key)
    return jnp.stack([fields[0], fields[1]], 0).astype(jnp.bfloat16)


def draw_cache_scale(key, part):
    return cache_fields(key)[2].astype(jnp.bfloat16)


def draw_offsets(key, part):
    return layout(key)[0]


def draw_lengths(key, part):
    return layout(key)[1]


def levels(own_key, extent, shards, least, largest):
    gain, own = 1.0, jax.random.fold_in(own_key, 6)
    for dim, blocks in shards:
        steps = jnp.exp(jax.random.uniform(jax.random.fold_in(own, dim), (blocks,), jnp.float32, least / len(shards), largest / len(shards)))
        gain = gain * jnp.repeat(steps, extent[dim] // blocks).reshape([-1 if axis == dim else 1 for axis in range(len(extent))])
    return gain


def bell_draw(own_key, shape, scale, most, cuts=(), kind=jnp.bfloat16):
    drawn = scale * jax.random.normal(own_key, shape, jnp.float32)
    if cuts:
        drawn = drawn * levels(own_key, shape, cuts, -0.22, 0.18)
    return jnp.clip(drawn, -most, most).astype(kind)


def setup_inputs(seed: int = 0, part: int = 0) -> dict:
    splits = jax.random.split(jax.random.key(seed), 8)
    part_keys = jax.random.split(jax.random.fold_in(splits[7], part), 8)
    return {
        "queries": draw_queries(jax.random.fold_in(jax.random.fold_in(splits[7], part), 71), part),
        "cache": draw_cache(jax.random.fold_in(jax.random.fold_in(splits[7], part), 71), part),
        "cache_scale": draw_cache_scale(jax.random.fold_in(jax.random.fold_in(splits[7], part), 71), part),
        "offsets": draw_offsets(jax.random.fold_in(jax.random.fold_in(splits[7], part), 71), part),
        "lengths": draw_lengths(jax.random.fold_in(jax.random.fold_in(splits[7], part), 71), part),
        "clamp_code": jax.random.randint(part_keys[5], (1,), 512, 1536).astype(jnp.int32),
        "w_out": bell_draw(splits[6], (HEADS * HD, D), (HEADS * HD) ** -0.5, 0.125, ((0, 16),)),
    }


NEG_FILL = -1e+30

def hadamard(matrix_size):
    counter_index = jnp.arange(matrix_size, dtype=jnp.int32)
    common = counter_index[:, None] & counter_index[None, :]
    parity = jnp.zeros((matrix_size, matrix_size), jnp.int32)
    for bit_place in range(matrix_size.bit_length() - 1):
        parity = parity + (common >> bit_place & 1)
    return jnp.where(parity % 2 == 0, 1.0, -1.0).astype(jnp.float32)

def reference(queries, cache, cache_scale, offsets, lengths, clamp_code, w_out):
    tok_rows = REQS * SPAN
    per_group = HEADS // KVH
    token_ids = jnp.arange(tok_rows, dtype=jnp.int32)
    request = token_ids // SPAN
    within = token_ids % SPAN
    starts = offsets[request]
    last_pos = starts + lengths[request] - SPAN + within
    positions = jnp.arange(LEN, dtype=jnp.int32)
    visible = (positions[None, :] >= starts[:, None]) & (positions[None, :] <= last_pos[:, None])
    inv_root = 1.0 / math.sqrt(HD)

    def one_head(kv_index):
        col_left = (kv_index * HD).astype(jnp.int32)
        key_rows = lax.dynamic_slice_in_dim(cache[0], col_left, HD, 1).astype(jnp.float32)
        value_rows = lax.dynamic_slice_in_dim(cache[1], col_left, HD, 1).astype(jnp.float32)
        query_block = lax.dynamic_slice_in_dim(queries, (kv_index * per_group * HD).astype(jnp.int32), per_group * HD, 1)
        query_block = query_block.reshape(tok_rows, per_group, HD).astype(jnp.float32)
        key_scale = lax.dynamic_index_in_dim(cache_scale[0], kv_index, 0, keepdims=False).astype(jnp.float32)
        value_scale = lax.dynamic_index_in_dim(cache_scale[1], kv_index, 0, keepdims=False).astype(jnp.float32)
        scores = jnp.einsum('tjd,pd->jtp', query_block, key_rows)
        scores = scores * (key_scale * inv_root)[None, None, :]
        masked = jnp.where(visible[None], scores, NEG_FILL)
        row_max = lax.optimization_barrier(jnp.max(masked, axis=2))
        weights = jnp.where(visible[None], jnp.exp(masked - row_max[..., None]), 0.0)
        prob_rows = (weights * value_scale[None, None, :]).astype(jnp.bfloat16)
        numerator = jnp.einsum('jtp,pd->jtd', prob_rows.astype(jnp.float32), value_rows)
        denominator = lax.optimization_barrier(jnp.sum(weights, axis=2))
        return (numerator / denominator[..., None]).astype(jnp.bfloat16)
    attention = lax.map(one_head, jnp.arange(KVH, dtype=jnp.int32)).reshape(HEADS, tok_rows, HD)
    rotated = jnp.einsum('htd,de->hte', attention.astype(jnp.float32), hadamard(HD), precision=lax.Precision.HIGHEST)
    rotated = jnp.einsum('gh,hte->gte', hadamard(HEADS), rotated, precision=lax.Precision.HIGHEST)
    rotated = rotated / math.sqrt(HEADS * HD)
    clip_limit = clamp_code[0].astype(jnp.float32) / 1024.0
    clamped = jnp.clip(rotated, -clip_limit, clip_limit).astype(jnp.bfloat16)
    activation = clamped.transpose(1, 0, 2).reshape(tok_rows, HEADS * HD)
    projected = lax.dot_general(w_out, activation, (((0,), (1,)), ((), ())), preferred_element_type=jnp.float32)
    return projected.astype(jnp.bfloat16)
```

```python
import functools
import math

import jax
import jax.numpy as jnp
from jax import lax
from jax.experimental import pallas as pl
from jax.experimental.pallas import tpu as pltpu
from jax.sharding import PartitionSpec as P

SPAN = 64


NEG_FILL = -1e30


def hadamard(matrix_size):
    counter_index = jnp.arange(matrix_size, dtype=jnp.int32)
    common = counter_index[:, None] & counter_index[None, :]
    parity = jnp.zeros((matrix_size, matrix_size), jnp.int32)
    for bit_place in range(matrix_size.bit_length() - 1):
        parity = parity + (common >> bit_place & 1)
    return jnp.where(parity % 2 == 0, 1.0, -1.0).astype(jnp.float32)


def masked_scores(query_block, key_rows, key_scale, visible_tile, inv_root):
    scores = jnp.einsum("tjd,pd->jtp", query_block, key_rows, preferred_element_type=jnp.float32)
    scores = scores * (key_scale.astype(jnp.float32) * inv_root)[None, None, :]
    return jnp.where(visible_tile[None], scores, NEG_FILL)


def tile_sums(masked, row_max, visible_tile, value_scale, value_rows):
    weights = jnp.where(visible_tile[None], jnp.exp(masked - row_max[..., None]), 0.0)
    prob_rows = (weights * value_scale.astype(jnp.float32)[None, None, :]).astype(jnp.bfloat16)
    numerator = jnp.einsum("jtp,pd->jtd", prob_rows, value_rows, preferred_element_type=jnp.float32)
    return (numerator, jnp.sum(weights, axis=2))


def fused_kernel(
    n,
    queries,
    kv_own,
    offsets,
    lengths,
    clamp_code,
    w_out,
    out,
    kv_all,
    scores,
    att_all,
    mix_send,
    mix_recv,
    core_send,
    core_recv,
    y_send,
    y_recv,
    z_send,
    z_recv,
    kv_zsem,
    kv_ysem,
    kv_csem,
    kv_rsem,
    att_ssem,
    att_rsem,
    mix_ssem,
    mix_rsem,
    core_ssem,
    core_rsem,
    y_ssem,
    y_rsem,
    z_ssem,
    z_rsem,
):
    f32, bf16 = jnp.float32, jnp.bfloat16
    rows = n // 4
    tok_rows, head_dim = queries.shape
    local_len = (kv_own.shape[0] - 16) // 2
    scale_rows = local_len // head_dim
    cols = out.shape[0]
    me = lax.axis_index("head")
    z, y, c = lax.div(me, 4), lax.rem(lax.div(me, 2), 2), lax.rem(me, 2)

    def place(zz, yy, cc):
        return zz * 4 + yy * 2 + cc

    def z_at(step):
        return lax.rem(z + step, rows)

    y_peer, c_peer = place(z, 1 - y, c), place(z, y, 1 - c)
    peers = [place(z_at(d), y, c) for d in range(1, rows)] + [y_peer, c_peer]

    def remote(src, dst, ssem, rsem, peer):
        return pltpu.make_async_remote_copy(
            src_ref=src,
            dst_ref=dst,
            send_sem=ssem,
            recv_sem=rsem,
            device_id={"head": peer},
            device_id_type=pl.DeviceIdType.MESH,
        )

    barrier = pltpu.get_barrier_semaphore()
    for peer in peers:
        pl.semaphore_signal(
            barrier, inc=1, device_id={"head": peer}, device_id_type=pl.DeviceIdType.MESH
        )
    pl.semaphore_wait(barrier, len(peers))

    sent = []

    def send(*args):
        copy = remote(*args)
        copy.start()
        sent.append(copy)

    for d in range(1, rows):
        send(kv_own, kv_all.at[me], kv_zsem.at[d], kv_rsem.at[me], place(z_at(d), y, c))
    send(kv_own, kv_all.at[me], kv_ysem.at[0], kv_rsem.at[me], y_peer)
    send(kv_own, kv_all.at[me], kv_csem.at[0], kv_rsem.at[me], c_peer)

    def kv_wait(slot):
        remote(kv_all.at[slot], kv_all.at[slot], kv_zsem.at[0], kv_rsem.at[slot], c_peer).wait_recv()

    token = lax.broadcasted_iota(jnp.int32, (tok_rows, 1), 0)
    starts = jnp.zeros((tok_rows, 1), jnp.int32)
    ends = jnp.zeros((tok_rows, 1), jnp.int32)
    for r in range(tok_rows // SPAN):
        mine = (token >= r * SPAN) & (token < (r + 1) * SPAN)
        starts = jnp.where(mine, offsets[r], starts)
        ends = jnp.where(mine, offsets[r] + lengths[r] - SPAN + token - r * SPAN, ends)
    inv_root = 1.0 / math.sqrt(head_dim)
    lane = lax.broadcasted_iota(jnp.int32, (tok_rows, local_len), 1)

    def scale_line(block, which):
        first = 2 * local_len + which * scale_rows
        lines = block[2 * local_len : 2 * local_len + 16, :].astype(f32)
        at = first - 2 * local_len
        return jnp.concatenate([lines[at + i : at + i + 1, :] for i in range(scale_rows)], axis=1)

    order = []
    maxima = []

    def score_block(slot, block):
        keys = block[0:local_len, :]
        part = lax.dot_general(
            queries[...], keys, (((1,), (1,)), ((), ())), preferred_element_type=f32
        )
        part = part * (scale_line(block, 0) * inv_root)
        positions = slot * local_len + lane
        part = jnp.where((positions >= starts) & (positions <= ends), part, NEG_FILL)
        scores[len(order)] = part
        order.append(block)
        maxima.append(jnp.max(part, axis=1, keepdims=True))

    score_block(me, kv_own)
    for d in range(1, rows):
        slot = place(z_at(d), y, c)
        kv_wait(slot)
        send(kv_all.at[slot], kv_all.at[slot], kv_ysem.at[d], kv_rsem.at[slot], y_peer)
        send(kv_all.at[slot], kv_all.at[slot], kv_csem.at[d], kv_rsem.at[slot], c_peer)
        score_block(slot, kv_all.at[slot])
    for d in range(rows):
        slot = place(z_at(d), 1 - y, c)
        kv_wait(slot)
        send(kv_all.at[slot], kv_all.at[slot], kv_csem.at[rows + d], kv_rsem.at[slot], c_peer)
        score_block(slot, kv_all.at[slot])
    for yy in (y, 1 - y):
        for d in range(rows):
            slot = place(z_at(d), yy, 1 - c)
            kv_wait(slot)
            score_block(slot, kv_all.at[slot])

    row_max = functools.reduce(jnp.maximum, maxima)
    numerator = jnp.zeros((tok_rows, head_dim), f32)
    denominator = jnp.zeros((tok_rows, 1), f32)
    for step, block in enumerate(order):
        weights = jnp.exp(scores[step] - row_max)
        denominator = denominator + jnp.sum(weights, axis=1, keepdims=True)
        probs = (weights * scale_line(block, 1)).astype(bf16)
        numerator = numerator + jnp.dot(
            probs, block[local_len : 2 * local_len, :], preferred_element_type=f32
        )
    att_all[z] = (numerator / denominator).astype(bf16)

    for d in range(1, rows):
        send(att_all.at[z], att_all.at[z], att_ssem.at[d], att_rsem.at[z], place(z_at(d), y, c))
    down = lax.broadcasted_iota(jnp.int32, (head_dim, head_dim), 0)
    across = lax.broadcasted_iota(jnp.int32, (head_dim, head_dim), 1)
    common = down & across
    parity = jnp.zeros((head_dim, head_dim), jnp.int32)
    for bit in range(head_dim.bit_length() - 1):
        parity = parity + ((common >> bit) & 1)
    hd_matrix = jnp.where((parity & 1) == 0, 1.0, -1.0).astype(f32)
    for d in range(1, rows):
        zz = z_at(d)
        remote(att_all.at[zz], att_all.at[zz], att_ssem.at[0], att_rsem.at[zz], y_peer).wait_recv()
    mixed = jnp.zeros((tok_rows, head_dim), f32)
    for zz in range(rows):
        odd = 0
        for bit in range(rows.bit_length() - 1):
            if zz >> bit & 1:
                odd = odd + lax.rem(lax.div(z, 1 << bit), 2)
        sign = (1 - 2 * lax.rem(odd, 2)).astype(f32) if zz else 1.0
        mixed = mixed + att_all[zz].astype(f32) * sign
    for level, (peer, bit) in enumerate(((y_peer, y), (c_peer, c))):
        mix_send[level] = mixed
        send(mix_send.at[level], mix_recv.at[level], mix_ssem.at[level], mix_rsem.at[level], peer)
        sign = (1 - 2 * bit).astype(f32)
        remote(
            mix_send.at[level], mix_recv.at[level], mix_ssem.at[level], mix_rsem.at[level], peer
        ).wait_recv()
        mixed = mixed * sign + mix_recv[level]
    rotated = jnp.dot(
        mixed, hd_matrix, precision=lax.Precision.HIGHEST, preferred_element_type=f32
    ) * (1.0 / math.sqrt(n * head_dim))
    limit = clamp_code[0].astype(f32) / 1024.0
    act = jnp.clip(rotated, -limit, limit).astype(bf16)

    def partial_sum(dest):
        columns = pl.ds(pl.multiple_of(dest * cols, cols), cols)
        return jnp.dot(act, w_out[:, columns], preferred_element_type=f32)

    steps = [d for d in range(1, rows)] + [0]
    for half, yy in enumerate((1 - y, y)):
        for d in steps:
            k = half * rows + d
            core_send[k] = partial_sum(place(z_at(d), yy, 1 - c)).astype(bf16)
            send(core_send.at[k], core_recv.at[k], core_ssem.at[k], core_rsem.at[k], c_peer)
        if half == 0:
            for d in steps:
                total = partial_sum(place(z_at(d), yy, c))
                remote(
                    core_send.at[d], core_recv.at[d], core_ssem.at[d], core_rsem.at[d], c_peer
                ).wait_recv()
                y_send[d] = (total + core_recv[d].astype(f32)).astype(bf16)
                send(y_send.at[d], y_recv.at[d], y_ssem.at[d], y_rsem.at[d], y_peer)
    total = None
    for d in steps:
        k = rows + d
        total = partial_sum(place(z_at(d), y, c))
        remote(
            core_send.at[k], core_recv.at[k], core_ssem.at[k], core_rsem.at[k], c_peer
        ).wait_recv()
        total = total + core_recv[k].astype(f32)
        remote(y_send.at[d], y_recv.at[d], y_ssem.at[d], y_rsem.at[d], y_peer).wait_recv()
        total = total + y_recv[d].astype(f32)
        if d:
            z_send[d] = total.astype(bf16)
            send(z_send.at[d], z_recv.at[d], z_ssem.at[d], z_rsem.at[d], place(z_at(d), y, c))
    for d in range(1, rows):
        remote(z_send.at[d], z_recv.at[d], z_ssem.at[d], z_rsem.at[d], y_peer).wait_recv()
        total = total + z_recv[d].astype(f32)
    out[...] = total.T.astype(out.dtype)
    for copy in sent:
        copy.wait_send()


def fused(n, queries, cache, cache_scale, offsets, lengths, clamp_code, w_out):
    tok_rows, head_dim = queries.shape
    local_len = cache.shape[1]
    rows = n // 4
    cols = w_out.shape[1] // n
    scale_rows = 2 * local_len // head_dim
    kv_own = jnp.concatenate(
        [
            cache.reshape(2 * local_len, head_dim),
            cache_scale.reshape(scale_rows, head_dim),
            jnp.zeros((16 - scale_rows, head_dim), cache.dtype),
        ],
        0,
    )
    vmem = pl.BlockSpec(memory_space=pltpu.VMEM)
    smem = pl.BlockSpec(memory_space=pltpu.SMEM)
    bf16, f32 = jnp.bfloat16, jnp.float32
    dma = pltpu.SemaphoreType.DMA
    block = (tok_rows, cols)
    return pl.pallas_call(
        functools.partial(fused_kernel, n),
        out_shape=jax.ShapeDtypeStruct((cols, tok_rows), bf16),
        in_specs=[vmem, vmem, smem, smem, smem, vmem],
        out_specs=vmem,
        scratch_shapes=[
            pltpu.VMEM((n,) + kv_own.shape, bf16),
            pltpu.VMEM((n, tok_rows, local_len), f32),
            pltpu.VMEM((rows, tok_rows, head_dim), bf16),
            pltpu.VMEM((2, tok_rows, head_dim), f32),
            pltpu.VMEM((2, tok_rows, head_dim), f32),
            pltpu.VMEM((2 * rows,) + block, bf16),
            pltpu.VMEM((2 * rows,) + block, bf16),
            pltpu.VMEM((rows,) + block, bf16),
            pltpu.VMEM((rows,) + block, bf16),
            pltpu.VMEM((rows,) + block, bf16),
            pltpu.VMEM((rows,) + block, bf16),
            dma((rows,)),
            dma((rows,)),
            dma((2 * rows,)),
            dma((n,)),
            dma((rows,)),
            dma((rows,)),
            dma((2,)),
            dma((2,)),
            dma((2 * rows,)),
            dma((2 * rows,)),
            dma((rows,)),
            dma((rows,)),
            dma((rows,)),
            dma((rows,)),
        ],
        compiler_params=pltpu.CompilerParams(
            collective_id=0, has_side_effects=True, vmem_limit_bytes=40 * 1024 * 1024
        ),
        cost_estimate=pl.CostEstimate(
            flops=2 * tok_rows * head_dim * (2 * n * local_len + w_out.shape[1]),
            bytes_accessed=2 * w_out.size + 2 * cols * tok_rows,
            transcendentals=tok_rows * n * local_len,
        ),
    )(queries, kv_own, offsets, lengths, clamp_code, w_out)


def fits_fused(n, queries, cache, w_out):
    head_dim, local_len = queries.shape[1], cache.shape[1]
    return (
        cache.shape[2] == head_dim
        and n % 4 == 0
        and (n & (n - 1)) == 0
        and local_len % head_dim == 0
        and 2 * local_len // head_dim <= 16
        and w_out.shape[1] % (n * 128) == 0
        and n * local_len <= 16384
    )


def per_device(n, queries, cache, cache_scale, offsets, lengths, clamp_code, w_out):
    if fits_fused(n, queries, cache, w_out):
        return fused(n, queries, cache, cache_scale, offsets, lengths, clamp_code, w_out)
    my_index = lax.axis_index("head")
    head_dim = queries.shape[1]
    local_len = cache.shape[1]
    kv_count = cache.shape[2] // head_dim
    gathered = lax.all_gather(queries, "head", axis=1, tiled=True)
    tok_rows = gathered.shape[0]
    head_count = gathered.shape[1] // head_dim
    per_group = head_count // kv_count
    token_ids = jnp.arange(tok_rows, dtype=jnp.int32)
    request = token_ids // SPAN
    within = token_ids % SPAN
    req_match = request[:, None] == jnp.arange(offsets.shape[0], dtype=jnp.int32)[None, :]
    starts = jnp.sum(jnp.where(req_match, offsets[None, :], 0), axis=1)
    last_pos = starts + jnp.sum(jnp.where(req_match, lengths[None, :], 0), axis=1) - SPAN + within
    inv_root = 1.0 / math.sqrt(head_dim)
    positions = my_index * local_len + jnp.arange(local_len, dtype=jnp.int32)
    visible = (positions[None, :] >= starts[:, None]) & (positions[None, :] <= last_pos[:, None])
    max_parts = []
    for kv_index in range(kv_count):
        column_left = kv_index * head_dim
        query_block = gathered[
            :, column_left * per_group : (column_left + head_dim) * per_group
        ].reshape(tok_rows, per_group, head_dim)
        masked = masked_scores(
            query_block,
            cache[0, :, column_left : column_left + head_dim],
            cache_scale[0, kv_index],
            visible,
            inv_root,
        )
        max_parts.append(jnp.max(masked, axis=2))
    local_max = jnp.concatenate(max_parts, 0)
    global_max = lax.pmax(local_max, "head")
    numer_parts = []
    denom_parts = []
    for kv_index in range(kv_count):
        column_left = kv_index * head_dim
        query_block = gathered[
            :, column_left * per_group : (column_left + head_dim) * per_group
        ].reshape(tok_rows, per_group, head_dim)
        masked = masked_scores(
            query_block,
            cache[0, :, column_left : column_left + head_dim],
            cache_scale[0, kv_index],
            visible,
            inv_root,
        )
        row_max = global_max[kv_index * per_group : (kv_index + 1) * per_group]
        numer_part, denom_part = tile_sums(
            masked,
            row_max,
            visible,
            cache_scale[1, kv_index],
            cache[1, :, column_left : column_left + head_dim],
        )
        numer_parts.append(numer_part)
        denom_parts.append(denom_part)
    numerator = jnp.concatenate(numer_parts, 0)
    denominator = jnp.concatenate(denom_parts, 0)
    numer_rows, denom_rows = (
        lax.psum_scatter(numerator, "head", scatter_dimension=1, tiled=True),
        lax.psum_scatter(denominator, "head", scatter_dimension=1, tiled=True),
    )
    token_attention = (numer_rows / denom_rows[..., None]).astype(jnp.bfloat16)
    clip_limit = clamp_code[0].astype(jnp.float32) / 1024.0
    scale_out = 1.0 / math.sqrt(head_count * head_dim)
    hd_matrix = hadamard(head_dim).astype(jnp.bfloat16)
    inner_mixed = jnp.einsum(
        "hrd,de->hre", token_attention, hd_matrix, preferred_element_type=jnp.float32
    )
    rotated = jnp.einsum(
        "gh,hre->gre", hadamard(head_count), inner_mixed, precision=lax.Precision.HIGHEST
    )
    clamped = jnp.clip(rotated * scale_out, -clip_limit, clip_limit).astype(jnp.bfloat16)
    activation = lax.all_to_all(clamped, "head", split_axis=0, concat_axis=1, tiled=True)[0]
    projected = lax.psum_scatter(
        lax.dot_general(
            w_out, activation, (((0,), (1,)), ((), ())), preferred_element_type=jnp.float32
        ),
        "head",
        scatter_dimension=0,
        tiled=True,
    )
    return projected.astype(jnp.bfloat16)


def solution(mesh):
    return jax.shard_map(
        functools.partial(per_device, mesh.shape["head"]),
        mesh=mesh,
        in_specs=(
            P("groups", "head"),
            P(None, ("groups", "head"), None),
            P(None, None, ("groups", "head")),
            P("groups"),
            P("groups"),
            P("groups"),
            P("head", None),
        ),
        out_specs=P("head", "groups"),
        check_vma=False,
    )
```

```python
import functools
import math

import jax
import jax.numpy as jnp
from jax import lax
from jax.experimental import pallas as pl
from jax.experimental.pallas import tpu as pltpu
from jax.sharding import PartitionSpec as P

SPAN = 64


NEG_FILL = -1e30

EARLY = 2


def hadamard(matrix_size):
    counter_index = jnp.arange(matrix_size, dtype=jnp.int32)
    common = counter_index[:, None] & counter_index[None, :]
    parity = jnp.zeros((matrix_size, matrix_size), jnp.int32)
    for bit_place in range(matrix_size.bit_length() - 1):
        parity = parity + (common >> bit_place & 1)
    return jnp.where(parity % 2 == 0, 1.0, -1.0).astype(jnp.float32)


def masked_scores(query_block, key_rows, key_scale, visible_tile, inv_root):
    scores = jnp.einsum("tjd,pd->jtp", query_block, key_rows, preferred_element_type=jnp.float32)
    scores = scores * (key_scale.astype(jnp.float32) * inv_root)[None, None, :]
    return jnp.where(visible_tile[None], scores, NEG_FILL)


def tile_sums(masked, row_max, visible_tile, value_scale, value_rows):
    weights = jnp.where(visible_tile[None], jnp.exp(masked - row_max[..., None]), 0.0)
    prob_rows = (weights * value_scale.astype(jnp.float32)[None, None, :]).astype(jnp.bfloat16)
    numerator = jnp.einsum("jtp,pd->jtd", prob_rows, value_rows, preferred_element_type=jnp.float32)
    return (numerator, jnp.sum(weights, axis=2))


def fused_kernel(
    n,
    queries_hbm,
    cache_hbm,
    scale_hbm,
    offsets_hbm,
    lengths_hbm,
    clamp_hbm,
    w_out,
    out,
    queries,
    kv_own,
    scale_own,
    offsets,
    lengths,
    clamp_code,
    w_own,
    w_quad,
    kv_all,
    scores,
    att_all,
    mix_send,
    mix_recv,
    z_send,
    z_recv,
    own_sem,
    w_sem,
    wq_ssem,
    wq_rsem,
    wx_ssem,
    wx_rsem,
    kv_zsem,
    kv_ysem,
    kv_csem,
    kv_rsem,
    att_ssem,
    att_rsem,
    mix_ssem,
    mix_rsem,
    z_ssem,
    z_rsem,
):
    f32, bf16 = jnp.float32, jnp.bfloat16
    rows = n // 4
    tok_rows, head_dim = queries.shape
    half_dim = head_dim // 2
    local_len = (kv_own.shape[0] - 16) // 2
    scale_rows = local_len // head_dim
    cols = out.shape[0]
    me = lax.axis_index("head")
    group = lax.axis_index("groups")
    z, y, c = lax.div(me, 4), lax.rem(lax.div(me, 2), 2), lax.rem(me, 2)

    def place(zz, yy, cc):
        return zz * 4 + yy * 2 + cc

    def z_at(step):
        return lax.rem(z + step, rows)

    y_peer, c_peer = place(z, 1 - y, c), place(z, y, 1 - c)
    quad = (place(z, y, c), c_peer, y_peer, place(z, 1 - y, 1 - c))
    peers = [place(z_at(d), y, c) for d in range(1, rows)] + list(quad[1:])

    locals_in = (
        (cache_hbm.at[0], kv_own.at[pl.ds(0, local_len)]),
        (cache_hbm.at[1], kv_own.at[pl.ds(local_len, local_len)]),
        (scale_hbm, scale_own),
        (queries_hbm, queries),
        (offsets_hbm, offsets),
        (lengths_hbm, lengths),
        (clamp_hbm, clamp_code),
    )
    own_copies = [
        pltpu.make_async_copy(src, dst, own_sem.at[i]) for i, (src, dst) in enumerate(locals_in)
    ]
    for copy in own_copies:
        copy.start()

    def remote(src, dst, ssem, rsem, peer, to_group=None):
        target = {"head": peer}
        if to_group is not None:
            target["groups"] = to_group
        return pltpu.make_async_remote_copy(
            src_ref=src,
            dst_ref=dst,
            send_sem=ssem,
            recv_sem=rsem,
            device_id=target,
            device_id_type=pl.DeviceIdType.MESH,
        )

    barrier = pltpu.get_barrier_semaphore()
    for peer in peers:
        pl.semaphore_signal(
            barrier, inc=1, device_id={"head": peer}, device_id_type=pl.DeviceIdType.MESH
        )
    pl.semaphore_signal(
        barrier,
        inc=1,
        device_id={"head": me, "groups": 1 - group},
        device_id_type=pl.DeviceIdType.MESH,
    )
    for copy in own_copies[:3]:
        copy.wait()
    scale_lines = scale_own[...].astype(f32)
    lines = [
        scale_lines[which, :, i * head_dim : (i + 1) * head_dim]
        for which in range(2)
        for i in range(scale_rows)
    ]
    lines.append(jnp.zeros((16 - len(lines), head_dim), f32))
    kv_own[2 * local_len : 2 * local_len + 16, :] = jnp.concatenate(lines, axis=0).astype(bf16)
    pl.semaphore_wait(barrier, len(peers) + 1)

    sent = []

    def send(*args):
        copy = remote(*args)
        copy.start()
        sent.append(copy)

    for d in range(1, rows):
        send(kv_own, kv_all.at[me], kv_zsem.at[d], kv_rsem.at[me], place(z_at(d), y, c))
    send(kv_own, kv_all.at[me], kv_ysem.at[0], kv_rsem.at[me], y_peer)
    send(kv_own, kv_all.at[me], kv_csem.at[0], kv_rsem.at[me], c_peer)

    def w_columns(d, yy, cc):
        row = z_at(d - d % 2)
        row = row + (1 - 2 * lax.rem(row, 2)) * (d % 2)
        return pl.ds(pl.multiple_of(place(row, yy, cc) * cols, cols), cols)

    quad_at = ((y, c), (y, 1 - c), (1 - y, c), (1 - y, 1 - c))
    my_half = pl.ds(pl.multiple_of(group * half_dim, half_dim), half_dim)

    other_half = pl.ds(pl.multiple_of((1 - group) * half_dim, half_dim), half_dim)

    def w_share(d):
        for k in (2, 3):
            send(
                w_out.at[my_half, w_columns(d, *quad_at[k])],
                w_quad.at[k - 1, d, my_half],
                wq_ssem.at[k - 1, d],
                wq_rsem.at[k - 1, d],
                quad[k],
            )

    def w_core(d):
        send(
            w_out.at[:, w_columns(d, *quad_at[1])],
            w_quad.at[0, d],
            wq_ssem.at[0, d],
            wq_rsem.at[0, d],
            quad[1],
        )

    def w_forward(d):
        for k in (1, 2):
            mine = w_quad.at[k, d, my_half]
            remote(mine, mine, wq_ssem.at[k, d], wq_rsem.at[k, d], y_peer).wait_recv()
            send(mine, mine, wx_ssem.at[k, d], wx_rsem.at[k, d], me, 1 - group)

    def w_wait(d):
        full = w_quad.at[0, d]
        remote(full, full, wq_ssem.at[0, d], wq_rsem.at[0, d], y_peer).wait_recv()
        for k in (1, 2):
            half = w_quad.at[k, d, other_half]
            remote(half, half, wx_ssem.at[k, d], wx_rsem.at[k, d], me, 1 - group).wait_recv()

    steps = [d for p in range(1, rows // 2) for d in (2 * p + 1, 2 * p)] + [1, 0]
    w_copies = [
        pltpu.make_async_copy(w_out.at[:, w_columns(d, y, c)], w_own.at[d], w_sem.at[d])
        for d in range(rows)
    ]
    for copy in w_copies:
        copy.start()
    for d in steps[:EARLY]:
        w_share(d)
    for d in steps:
        w_core(d)

    def kv_wait(slot):
        remote(kv_all.at[slot], kv_all.at[slot], kv_zsem.at[0], kv_rsem.at[slot], c_peer).wait_recv()

    for copy in own_copies[3:]:
        copy.wait()
    token = lax.broadcasted_iota(jnp.int32, (tok_rows, 1), 0)
    starts = jnp.zeros((tok_rows, 1), jnp.int32)
    ends = jnp.zeros((tok_rows, 1), jnp.int32)
    for r in range(tok_rows // SPAN):
        mine = (token >= r * SPAN) & (token < (r + 1) * SPAN)
        starts = jnp.where(mine, offsets[r], starts)
        ends = jnp.where(mine, offsets[r] + lengths[r] - SPAN + token - r * SPAN, ends)
    inv_root = 1.0 / math.sqrt(head_dim)
    lane = lax.broadcasted_iota(jnp.int32, (tok_rows, local_len), 1)

    def scale_line(block, which):
        first = 2 * local_len + which * scale_rows
        lines = block[2 * local_len : 2 * local_len + 16, :].astype(f32)
        at = first - 2 * local_len
        return jnp.concatenate([lines[at + i : at + i + 1, :] for i in range(scale_rows)], axis=1)

    order = []
    maxima = []

    def score_block(slot, block):
        keys = block[0:local_len, :]
        part = lax.dot_general(
            queries[...], keys, (((1,), (1,)), ((), ())), preferred_element_type=f32
        )
        part = part * (scale_line(block, 0) * inv_root)
        positions = slot * local_len + lane
        part = jnp.where((positions >= starts) & (positions <= ends), part, NEG_FILL)
        scores[len(order)] = part
        order.append(block)
        maxima.append(jnp.max(part, axis=1, keepdims=True))

    score_block(me, kv_own)
    for d in range(1, rows):
        slot = place(z_at(d), y, c)
        kv_wait(slot)
        send(kv_all.at[slot], kv_all.at[slot], kv_ysem.at[d], kv_rsem.at[slot], y_peer)
        send(kv_all.at[slot], kv_all.at[slot], kv_csem.at[d], kv_rsem.at[slot], c_peer)
        score_block(slot, kv_all.at[slot])
    for d in range(rows):
        slot = place(z_at(d), 1 - y, c)
        kv_wait(slot)
        send(kv_all.at[slot], kv_all.at[slot], kv_csem.at[rows + d], kv_rsem.at[slot], c_peer)
        score_block(slot, kv_all.at[slot])
    for d in steps[EARLY:]:
        w_share(d)
    for d in steps[:EARLY]:
        w_forward(d)
    for yy in (y, 1 - y):
        for d in range(rows):
            slot = place(z_at(d), yy, 1 - c)
            kv_wait(slot)
            score_block(slot, kv_all.at[slot])

    row_max = functools.reduce(jnp.maximum, maxima)
    numerator = jnp.zeros((tok_rows, head_dim), f32)
    denominator = jnp.zeros((tok_rows, 1), f32)
    for step, block in enumerate(order):
        weights = jnp.exp(scores[step] - row_max)
        denominator = denominator + jnp.sum(weights, axis=1, keepdims=True)
        probs = (weights * scale_line(block, 1)).astype(bf16)
        numerator = numerator + jnp.dot(
            probs, block[local_len : 2 * local_len, :], preferred_element_type=f32
        )
    att_all[z] = (numerator / denominator).astype(bf16)

    for d in range(1, rows):
        send(att_all.at[z], att_all.at[z], att_ssem.at[d], att_rsem.at[z], place(z_at(d), y, c))
    for d in steps[EARLY:3]:
        w_forward(d)
    down = lax.broadcasted_iota(jnp.int32, (head_dim, head_dim), 0)
    across = lax.broadcasted_iota(jnp.int32, (head_dim, head_dim), 1)
    common = down & across
    parity = jnp.zeros((head_dim, head_dim), jnp.int32)
    for bit in range(head_dim.bit_length() - 1):
        parity = parity + ((common >> bit) & 1)
    hd_matrix = jnp.where((parity & 1) == 0, 1.0, -1.0).astype(f32)
    for d in range(1, rows):
        zz = z_at(d)
        remote(att_all.at[zz], att_all.at[zz], att_ssem.at[0], att_rsem.at[zz], y_peer).wait_recv()
    mixed = jnp.zeros((tok_rows, head_dim), f32)
    for zz in range(rows):
        odd = 0
        for bit in range(rows.bit_length() - 1):
            if zz >> bit & 1:
                odd = odd + lax.rem(lax.div(z, 1 << bit), 2)
        sign = (1 - 2 * lax.rem(odd, 2)).astype(f32) if zz else 1.0
        mixed = mixed + att_all[zz].astype(f32) * sign
    mixed = jnp.dot(mixed, hd_matrix, precision=lax.Precision.HIGHEST, preferred_element_type=f32)

    def swap(at, size, level, peer):
        there = remote(
            mix_send.at[pl.ds(at, size)],
            mix_recv.at[pl.ds(at, size)],
            mix_ssem.at[level],
            mix_rsem.at[level],
            peer,
        )
        there.start()
        sent.append(there)
        return there

    mix_send[0] = mixed
    there = swap(0, 1, 0, y_peer)
    for d in steps[max(EARLY, 3):]:
        w_forward(d)
    there.wait_recv()
    y_sign, c_sign = (1 - 2 * y).astype(f32), (1 - 2 * c).astype(f32)
    pair = (mixed * y_sign + mix_recv[0], mixed - mix_recv[0] * y_sign)
    mix_send[1] = pair[0]
    mix_send[2] = pair[1]
    there = swap(1, 2, 1, c_peer)
    there.wait_recv()
    limit = clamp_code[0].astype(f32) / 1024.0
    scale_out = 1.0 / math.sqrt(n * head_dim)
    acts = []
    for i in range(2):
        for full in (pair[i] * c_sign + mix_recv[1 + i], pair[i] - mix_recv[1 + i] * c_sign):
            acts.append(jnp.clip(full * scale_out, -limit, limit).astype(bf16))

    def row_sum(d):
        w_copies[d].wait()
        w_wait(d)
        total = jnp.dot(acts[0], w_own[d], preferred_element_type=f32)
        for k in range(3):
            total = total + jnp.dot(acts[k + 1], w_quad[k, d], preferred_element_type=f32)
        return total

    def z_wait(slot, peer):
        remote(
            z_send.at[slot], z_recv.at[slot], z_ssem.at[slot], z_rsem.at[slot], peer
        ).wait_recv()
        return z_recv[slot].astype(f32)

    def z_go(slot, value, peer):
        z_send[slot] = value.astype(bf16)
        send(z_send.at[slot], z_recv.at[slot], z_ssem.at[slot], z_rsem.at[slot], peer)

    far = rows // 2 - 1
    low = lax.rem(z, 2)
    z_mate = place(z + 1 - 2 * low, y, c)
    for p in range(1, far + 1):
        z_go(p - 1, row_sum(2 * p + 1), z_mate)
    kept = [row_sum(2 * p) for p in range(1, far + 1)]
    near = row_sum(1)
    for p in range(1, far + 1):
        peer = place(z_at(2 * p), y, c)
        z_go(far + p - 1, kept[p - 1] + z_wait(p - 1, z_mate), peer)
    z_go(2 * far, near, z_mate)
    total = row_sum(0)
    total = total + z_wait(2 * far, z_mate)
    for p in range(1, far + 1):
        total = total + z_wait(far + p - 1, z_mate)
    out[...] = total.T.astype(out.dtype)
    for copy in sent:
        copy.wait_send()


def fused(n, queries, cache, cache_scale, offsets, lengths, clamp_code, w_out):
    tok_rows, head_dim = queries.shape
    local_len = cache.shape[1]
    rows = n // 4
    cols = w_out.shape[1] // n
    kv_shape = (2 * local_len + 16, head_dim)
    vmem = pl.BlockSpec(memory_space=pltpu.VMEM)
    hbm = pl.BlockSpec(memory_space=pltpu.HBM)
    bf16, f32 = jnp.bfloat16, jnp.float32
    dma = pltpu.SemaphoreType.DMA
    block = (tok_rows, cols)
    return pl.pallas_call(
        functools.partial(fused_kernel, n),
        out_shape=jax.ShapeDtypeStruct((cols, tok_rows), bf16),
        in_specs=[hbm] * 7,
        out_specs=vmem,
        scratch_shapes=[
            pltpu.VMEM(queries.shape, bf16),
            pltpu.VMEM(kv_shape, bf16),
            pltpu.VMEM(cache_scale.shape, bf16),
            pltpu.SMEM(offsets.shape, jnp.int32),
            pltpu.SMEM(lengths.shape, jnp.int32),
            pltpu.SMEM(clamp_code.shape, jnp.int32),
            pltpu.VMEM((rows, head_dim, cols), bf16),
            pltpu.VMEM((3, rows, head_dim, cols), bf16),
            pltpu.VMEM((n,) + kv_shape, bf16),
            pltpu.VMEM((n, tok_rows, local_len), f32),
            pltpu.VMEM((rows, tok_rows, head_dim), bf16),
            pltpu.VMEM((3, tok_rows, head_dim), f32),
            pltpu.VMEM((3, tok_rows, head_dim), f32),
            pltpu.VMEM((rows,) + block, bf16),
            pltpu.VMEM((rows,) + block, bf16),
            dma((7,)),
            dma((rows,)),
            dma((3, rows)),
            dma((3, rows)),
            dma((3, rows)),
            dma((3, rows)),
            dma((rows,)),
            dma((rows,)),
            dma((2 * rows,)),
            dma((n,)),
            dma((rows,)),
            dma((rows,)),
            dma((2,)),
            dma((2,)),
            dma((rows,)),
            dma((rows,)),
        ],
        compiler_params=pltpu.CompilerParams(
            collective_id=0, has_side_effects=True, vmem_limit_bytes=40 * 1024 * 1024
        ),
        cost_estimate=pl.CostEstimate(
            flops=2 * tok_rows * head_dim * (2 * n * local_len + w_out.shape[1]),
            bytes_accessed=2 * w_out.size + 2 * cols * tok_rows,
            transcendentals=tok_rows * n * local_len,
        ),
    )(queries, cache, cache_scale, offsets, lengths, clamp_code, w_out)


def fits_fused(groups, n, queries, cache, w_out):
    head_dim, local_len = queries.shape[1], cache.shape[1]
    return (
        groups == 2
        and cache.shape[2] == head_dim
        and head_dim % 32 == 0
        and n % 4 == 0
        and n >= 16
        and (n & (n - 1)) == 0
        and local_len % head_dim == 0
        and 2 * local_len // head_dim <= 16
        and w_out.shape[1] % (n * 128) == 0
        and n * local_len <= 16384
    )


def per_device(groups, n, queries, cache, cache_scale, offsets, lengths, clamp_code, w_out):
    if fits_fused(groups, n, queries, cache, w_out):
        return fused(n, queries, cache, cache_scale, offsets, lengths, clamp_code, w_out)
    my_index = lax.axis_index("head")
    head_dim = queries.shape[1]
    local_len = cache.shape[1]
    kv_count = cache.shape[2] // head_dim
    gathered = lax.all_gather(queries, "head", axis=1, tiled=True)
    tok_rows = gathered.shape[0]
    head_count = gathered.shape[1] // head_dim
    per_group = head_count // kv_count
    token_ids = jnp.arange(tok_rows, dtype=jnp.int32)
    request = token_ids // SPAN
    within = token_ids % SPAN
    req_match = request[:, None] == jnp.arange(offsets.shape[0], dtype=jnp.int32)[None, :]
    starts = jnp.sum(jnp.where(req_match, offsets[None, :], 0), axis=1)
    last_pos = starts + jnp.sum(jnp.where(req_match, lengths[None, :], 0), axis=1) - SPAN + within
    inv_root = 1.0 / math.sqrt(head_dim)
    positions = my_index * local_len + jnp.arange(local_len, dtype=jnp.int32)
    visible = (positions[None, :] >= starts[:, None]) & (positions[None, :] <= last_pos[:, None])
    max_parts = []
    for kv_index in range(kv_count):
        column_left = kv_index * head_dim
        query_block = gathered[
            :, column_left * per_group : (column_left + head_dim) * per_group
        ].reshape(tok_rows, per_group, head_dim)
        masked = masked_scores(
            query_block,
            cache[0, :, column_left : column_left + head_dim],
            cache_scale[0, kv_index],
            visible,
            inv_root,
        )
        max_parts.append(jnp.max(masked, axis=2))
    local_max = jnp.concatenate(max_parts, 0)
    global_max = lax.pmax(local_max, "head")
    numer_parts = []
    denom_parts = []
    for kv_index in range(kv_count):
        column_left = kv_index * head_dim
        query_block = gathered[
            :, column_left * per_group : (column_left + head_dim) * per_group
        ].reshape(tok_rows, per_group, head_dim)
        masked = masked_scores(
            query_block,
            cache[0, :, column_left : column_left + head_dim],
            cache_scale[0, kv_index],
            visible,
            inv_root,
        )
        row_max = global_max[kv_index * per_group : (kv_index + 1) * per_group]
        numer_part, denom_part = tile_sums(
            masked,
            row_max,
            visible,
            cache_scale[1, kv_index],
            cache[1, :, column_left : column_left + head_dim],
        )
        numer_parts.append(numer_part)
        denom_parts.append(denom_part)
    numerator = jnp.concatenate(numer_parts, 0)
    denominator = jnp.concatenate(denom_parts, 0)
    numer_rows, denom_rows = (
        lax.psum_scatter(numerator, "head", scatter_dimension=1, tiled=True),
        lax.psum_scatter(denominator, "head", scatter_dimension=1, tiled=True),
    )
    token_attention = (numer_rows / denom_rows[..., None]).astype(jnp.bfloat16)
    clip_limit = clamp_code[0].astype(jnp.float32) / 1024.0
    scale_out = 1.0 / math.sqrt(head_count * head_dim)
    hd_matrix = hadamard(head_dim).astype(jnp.bfloat16)
    inner_mixed = jnp.einsum(
        "hrd,de->hre", token_attention, hd_matrix, preferred_element_type=jnp.float32
    )
    rotated = jnp.einsum(
        "gh,hre->gre", hadamard(head_count), inner_mixed, precision=lax.Precision.HIGHEST
    )
    clamped = jnp.clip(rotated * scale_out, -clip_limit, clip_limit).astype(jnp.bfloat16)
    activation = lax.all_to_all(clamped, "head", split_axis=0, concat_axis=1, tiled=True)[0]
    projected = lax.psum_scatter(
        lax.dot_general(
            w_out, activation, (((0,), (1,)), ((), ())), preferred_element_type=jnp.float32
        ),
        "head",
        scatter_dimension=0,
        tiled=True,
    )
    return projected.astype(jnp.bfloat16)


def solution(mesh):
    return jax.shard_map(
        functools.partial(per_device, mesh.shape["groups"], mesh.shape["head"]),
        mesh=mesh,
        in_specs=(
            P("groups", "head"),
            P(None, ("groups", "head"), None),
            P(None, None, ("groups", "head")),
            P("groups"),
            P("groups"),
            P("groups"),
            P("head", None),
        ),
        out_specs=P("head", "groups"),
        check_vma=False,
    )
```

```python
import functools
import math

import jax
import jax.numpy as jnp
from jax import lax
from jax.experimental import pallas as pl
from jax.experimental.pallas import tpu as pltpu
from jax.sharding import PartitionSpec as P

SPAN = 64


NEG_FILL = -1e30

EARLY = 1

LATE = 2


def hadamard(matrix_size):
    counter_index = jnp.arange(matrix_size, dtype=jnp.int32)
    common = counter_index[:, None] & counter_index[None, :]
    parity = jnp.zeros((matrix_size, matrix_size), jnp.int32)
    for bit_place in range(matrix_size.bit_length() - 1):
        parity = parity + (common >> bit_place & 1)
    return jnp.where(parity % 2 == 0, 1.0, -1.0).astype(jnp.float32)


def masked_scores(query_block, key_rows, key_scale, visible_tile, inv_root):
    scores = jnp.einsum("tjd,pd->jtp", query_block, key_rows, preferred_element_type=jnp.float32)
    scores = scores * (key_scale.astype(jnp.float32) * inv_root)[None, None, :]
    return jnp.where(visible_tile[None], scores, NEG_FILL)


def tile_sums(masked, row_max, visible_tile, value_scale, value_rows):
    weights = jnp.where(visible_tile[None], jnp.exp(masked - row_max[..., None]), 0.0)
    prob_rows = (weights * value_scale.astype(jnp.float32)[None, None, :]).astype(jnp.bfloat16)
    numerator = jnp.einsum("jtp,pd->jtd", prob_rows, value_rows, preferred_element_type=jnp.float32)
    return (numerator, jnp.sum(weights, axis=2))


def fused_kernel(
    n,
    queries_hbm,
    cache_hbm,
    scale_hbm,
    offsets_hbm,
    lengths_hbm,
    clamp_hbm,
    w_out,
    out,
    queries,
    kv_own,
    scale_own,
    offsets,
    lengths,
    clamp_code,
    w_own,
    w_quad,
    kv_all,
    scores,
    att_all,
    mix_send,
    mix_recv,
    z_send,
    z_recv,
    y_send,
    y_recv,
    own_sem,
    w_sem,
    wq_ssem,
    wq_rsem,
    wx_ssem,
    wx_rsem,
    kv_zsem,
    kv_ysem,
    kv_csem,
    kv_rsem,
    att_ssem,
    att_rsem,
    mix_ssem,
    mix_rsem,
    z_ssem,
    z_rsem,
    y_ssem,
    y_rsem,
):
    f32, bf16 = jnp.float32, jnp.bfloat16
    rows = n // 4
    tok_rows, head_dim = queries.shape
    half_dim = head_dim // 2
    local_len = (kv_own.shape[0] - 16) // 2
    scale_rows = local_len // head_dim
    cols = out.shape[0]
    me = lax.axis_index("head")
    group = lax.axis_index("groups")
    z, y, c = lax.div(me, 4), lax.rem(lax.div(me, 2), 2), lax.rem(me, 2)

    def place(zz, yy, cc):
        return zz * 4 + yy * 2 + cc

    def z_at(step):
        return lax.rem(z + step, rows)

    y_peer, c_peer = place(z, 1 - y, c), place(z, y, 1 - c)
    quad = (place(z, y, c), c_peer, y_peer, place(z, 1 - y, 1 - c))
    peers = [place(z_at(d), y, c) for d in range(1, rows)] + list(quad[1:])

    locals_in = (
        (cache_hbm.at[0], kv_own.at[pl.ds(0, local_len)]),
        (cache_hbm.at[1], kv_own.at[pl.ds(local_len, local_len)]),
        (scale_hbm, scale_own),
        (queries_hbm, queries),
        (offsets_hbm, offsets),
        (lengths_hbm, lengths),
        (clamp_hbm, clamp_code),
    )
    own_copies = [
        pltpu.make_async_copy(src, dst, own_sem.at[i]) for i, (src, dst) in enumerate(locals_in)
    ]
    for copy in own_copies:
        copy.start()

    def remote(src, dst, ssem, rsem, peer, to_group=None):
        target = {"head": peer}
        if to_group is not None:
            target["groups"] = to_group
        return pltpu.make_async_remote_copy(
            src_ref=src,
            dst_ref=dst,
            send_sem=ssem,
            recv_sem=rsem,
            device_id=target,
            device_id_type=pl.DeviceIdType.MESH,
        )

    barrier = pltpu.get_barrier_semaphore()
    for peer in peers:
        pl.semaphore_signal(
            barrier, inc=1, device_id={"head": peer}, device_id_type=pl.DeviceIdType.MESH
        )
    pl.semaphore_signal(
        barrier,
        inc=1,
        device_id={"head": me, "groups": 1 - group},
        device_id_type=pl.DeviceIdType.MESH,
    )
    for copy in own_copies[:3]:
        copy.wait()
    scale_lines = scale_own[...].astype(f32)
    lines = [
        scale_lines[which, :, i * head_dim : (i + 1) * head_dim]
        for which in range(2)
        for i in range(scale_rows)
    ]
    lines.append(jnp.zeros((16 - len(lines), head_dim), f32))
    kv_own[2 * local_len : 2 * local_len + 16, :] = jnp.concatenate(lines, axis=0).astype(bf16)
    pl.semaphore_wait(barrier, len(peers) + 1)

    sent = []

    def send(*args):
        copy = remote(*args)
        copy.start()
        sent.append(copy)

    for d in range(1, rows):
        send(kv_own, kv_all.at[me], kv_zsem.at[d], kv_rsem.at[me], place(z_at(d), y, c))
    send(kv_own, kv_all.at[me], kv_ysem.at[0], kv_rsem.at[me], y_peer)
    send(kv_own, kv_all.at[me], kv_csem.at[0], kv_rsem.at[me], c_peer)

    def w_columns(d, yy, cc):
        row = z_at(d - d % 2)
        row = row + (1 - 2 * lax.rem(row, 2)) * (d % 2)
        return pl.ds(pl.multiple_of(place(row, yy, cc) * cols, cols), cols)

    quad_at = ((y, c), (y, 1 - c), (1 - y, c), (1 - y, 1 - c))
    my_half = pl.ds(pl.multiple_of(group * half_dim, half_dim), half_dim)

    other_half = pl.ds(pl.multiple_of((1 - group) * half_dim, half_dim), half_dim)

    def w_share(d):
        for k in (2, 3):
            send(
                w_out.at[my_half, w_columns(d, *quad_at[k])],
                w_quad.at[k - 1, d, my_half],
                wq_ssem.at[k - 1, d],
                wq_rsem.at[k - 1, d],
                quad[k],
            )

    def w_core(d):
        send(
            w_out.at[:, w_columns(d, *quad_at[1])],
            w_quad.at[0, d],
            wq_ssem.at[0, d],
            wq_rsem.at[0, d],
            quad[1],
        )

    def w_forward(d):
        for k in (1, 2):
            mine = w_quad.at[k, d, my_half]
            remote(mine, mine, wq_ssem.at[k, d], wq_rsem.at[k, d], y_peer).wait_recv()
            send(mine, mine, wx_ssem.at[k, d], wx_rsem.at[k, d], me, 1 - group)

    def w_wait(d):
        full = w_quad.at[0, d]
        remote(full, full, wq_ssem.at[0, d], wq_rsem.at[0, d], y_peer).wait_recv()
        for k in (1, 2) if d in shared else ():
            half = w_quad.at[k, d, other_half]
            remote(half, half, wx_ssem.at[k, d], wx_rsem.at[k, d], me, 1 - group).wait_recv()

    steps = [d for p in range(1, rows // 2) for d in (2 * p + 1, 2 * p)] + [1, 0]
    late = steps[len(steps) - LATE :]
    shared = steps[: len(steps) - LATE]
    w_copies = [
        pltpu.make_async_copy(w_out.at[:, w_columns(d, y, c)], w_own.at[d], w_sem.at[d])
        for d in range(rows)
    ]
    late_copies = {
        d: pltpu.make_async_copy(
            w_out.at[:, w_columns(d, 1 - y, c)], w_quad.at[1, d], w_sem.at[rows + d]
        )
        for d in late
    }
    for copy in w_copies + list(late_copies.values()):
        copy.start()
    for d in shared[:EARLY]:
        w_share(d)
    for d in steps:
        w_core(d)
    for d in late:
        send(
            w_out.at[:, w_columns(d, 1 - y, 1 - c)],
            w_quad.at[2, d],
            wq_ssem.at[2, d],
            wq_rsem.at[2, d],
            c_peer,
        )

    def kv_wait(slot):
        remote(kv_all.at[slot], kv_all.at[slot], kv_zsem.at[0], kv_rsem.at[slot], c_peer).wait_recv()

    for copy in own_copies[3:]:
        copy.wait()
    token = lax.broadcasted_iota(jnp.int32, (tok_rows, 1), 0)
    starts = jnp.zeros((tok_rows, 1), jnp.int32)
    ends = jnp.zeros((tok_rows, 1), jnp.int32)
    for r in range(tok_rows // SPAN):
        mine = (token >= r * SPAN) & (token < (r + 1) * SPAN)
        starts = jnp.where(mine, offsets[r], starts)
        ends = jnp.where(mine, offsets[r] + lengths[r] - SPAN + token - r * SPAN, ends)
    inv_root = 1.0 / math.sqrt(head_dim)
    lane = lax.broadcasted_iota(jnp.int32, (tok_rows, local_len), 1)

    def scale_line(block, which):
        first = 2 * local_len + which * scale_rows
        lines = block[2 * local_len : 2 * local_len + 16, :].astype(f32)
        at = first - 2 * local_len
        return jnp.concatenate([lines[at + i : at + i + 1, :] for i in range(scale_rows)], axis=1)

    order = []
    maxima = []

    def score_block(slot, block):
        keys = block[0:local_len, :]
        part = lax.dot_general(
            queries[...], keys, (((1,), (1,)), ((), ())), preferred_element_type=f32
        )
        part = part * (scale_line(block, 0) * inv_root)
        positions = slot * local_len + lane
        part = jnp.where((positions >= starts) & (positions <= ends), part, NEG_FILL)
        scores[len(order)] = part
        order.append(block)
        maxima.append(jnp.max(part, axis=1, keepdims=True))

    score_block(me, kv_own)
    for d in range(1, rows):
        slot = place(z_at(d), y, c)
        kv_wait(slot)
        send(kv_all.at[slot], kv_all.at[slot], kv_ysem.at[d], kv_rsem.at[slot], y_peer)
        send(kv_all.at[slot], kv_all.at[slot], kv_csem.at[d], kv_rsem.at[slot], c_peer)
        score_block(slot, kv_all.at[slot])
    for d in range(rows):
        slot = place(z_at(d), 1 - y, c)
        kv_wait(slot)
        send(kv_all.at[slot], kv_all.at[slot], kv_csem.at[rows + d], kv_rsem.at[slot], c_peer)
        score_block(slot, kv_all.at[slot])
    for d in shared[EARLY:]:
        w_share(d)
    for d in shared[:EARLY]:
        w_forward(d)
    for yy in (y, 1 - y):
        for d in range(rows):
            slot = place(z_at(d), yy, 1 - c)
            kv_wait(slot)
            score_block(slot, kv_all.at[slot])

    row_max = functools.reduce(jnp.maximum, maxima)
    numerator = jnp.zeros((tok_rows, head_dim), f32)
    denominator = jnp.zeros((tok_rows, 1), f32)
    for step, block in enumerate(order):
        weights = jnp.exp(scores[step] - row_max)
        denominator = denominator + jnp.sum(weights, axis=1, keepdims=True)
        probs = (weights * scale_line(block, 1)).astype(bf16)
        numerator = numerator + jnp.dot(
            probs, block[local_len : 2 * local_len, :], preferred_element_type=f32
        )
    att_all[z] = (numerator / denominator).astype(bf16)

    for d in range(1, rows):
        send(att_all.at[z], att_all.at[z], att_ssem.at[d], att_rsem.at[z], place(z_at(d), y, c))
    for d in shared[EARLY:3]:
        w_forward(d)
    down = lax.broadcasted_iota(jnp.int32, (head_dim, head_dim), 0)
    across = lax.broadcasted_iota(jnp.int32, (head_dim, head_dim), 1)
    common = down & across
    parity = jnp.zeros((head_dim, head_dim), jnp.int32)
    for bit in range(head_dim.bit_length() - 1):
        parity = parity + ((common >> bit) & 1)
    hd_matrix = jnp.where((parity & 1) == 0, 1.0, -1.0).astype(f32)
    for d in range(1, rows):
        zz = z_at(d)
        remote(att_all.at[zz], att_all.at[zz], att_ssem.at[0], att_rsem.at[zz], y_peer).wait_recv()
    mixed = jnp.zeros((tok_rows, head_dim), f32)
    for zz in range(rows):
        odd = 0
        for bit in range(rows.bit_length() - 1):
            if zz >> bit & 1:
                odd = odd + lax.rem(lax.div(z, 1 << bit), 2)
        sign = (1 - 2 * lax.rem(odd, 2)).astype(f32) if zz else 1.0
        mixed = mixed + att_all[zz].astype(f32) * sign
    mixed = jnp.dot(mixed, hd_matrix, precision=lax.Precision.HIGHEST, preferred_element_type=f32)

    def swap(at, size, level, peer):
        there = remote(
            mix_send.at[pl.ds(at, size)],
            mix_recv.at[pl.ds(at, size)],
            mix_ssem.at[level],
            mix_rsem.at[level],
            peer,
        )
        there.start()
        sent.append(there)
        return there

    mix_send[0] = mixed
    there = swap(0, 1, 0, y_peer)
    for d in shared[max(EARLY, 3):]:
        w_forward(d)
    there.wait_recv()
    y_sign, c_sign = (1 - 2 * y).astype(f32), (1 - 2 * c).astype(f32)
    pair = (mixed * y_sign + mix_recv[0], mixed - mix_recv[0] * y_sign)
    mix_send[1] = pair[0]
    mix_send[2] = pair[1]
    there = swap(1, 2, 1, c_peer)
    there.wait_recv()
    limit = clamp_code[0].astype(f32) / 1024.0
    scale_out = 1.0 / math.sqrt(n * head_dim)
    acts = []
    for i in range(2):
        for full in (pair[i] * c_sign + mix_recv[1 + i], pair[i] - mix_recv[1 + i] * c_sign):
            acts.append(jnp.clip(full * scale_out, -limit, limit).astype(bf16))

    def row_sum(d):
        w_copies[d].wait()
        w_wait(d)
        total = jnp.dot(acts[0], w_own[d], preferred_element_type=f32)
        if d in late:
            total = total + jnp.dot(acts[1], w_quad[0, d], preferred_element_type=f32)
            remote(y_send.at[d], y_recv.at[d], y_ssem.at[d], y_rsem.at[d], y_peer).wait_recv()
            return total + y_recv[d].astype(f32)
        for k in range(3):
            total = total + jnp.dot(acts[k + 1], w_quad[k, d], preferred_element_type=f32)
        return total

    def z_wait(slot, peer):
        remote(
            z_send.at[slot], z_recv.at[slot], z_ssem.at[slot], z_rsem.at[slot], peer
        ).wait_recv()
        return z_recv[slot].astype(f32)

    def z_go(slot, value, peer):
        z_send[slot] = value.astype(bf16)
        send(z_send.at[slot], z_recv.at[slot], z_ssem.at[slot], z_rsem.at[slot], peer)

    far = rows // 2 - 1
    low = lax.rem(z, 2)
    z_mate = place(z + 1 - 2 * low, y, c)
    for p in range(1, far + 1):
        z_go(p - 1, row_sum(2 * p + 1), z_mate)
    for d in late:
        late_copies[d].wait()
        full = w_quad.at[2, d]
        remote(full, full, wq_ssem.at[2, d], wq_rsem.at[2, d], c_peer).wait_recv()
        theirs = jnp.dot(acts[0], w_quad[1, d], preferred_element_type=f32)
        theirs = theirs + jnp.dot(acts[1], w_quad[2, d], preferred_element_type=f32)
        y_send[d] = theirs.astype(bf16)
        send(y_send.at[d], y_recv.at[d], y_ssem.at[d], y_rsem.at[d], y_peer)
    kept = [row_sum(2 * p) for p in range(1, far + 1)]
    near = row_sum(1)
    for p in range(1, far + 1):
        peer = place(z_at(2 * p), y, c)
        z_go(far + p - 1, kept[p - 1] + z_wait(p - 1, z_mate), peer)
    z_go(2 * far, near, z_mate)
    total = row_sum(0)
    total = total + z_wait(2 * far, z_mate)
    for p in range(1, far + 1):
        total = total + z_wait(far + p - 1, z_mate)
    out[...] = total.T.astype(out.dtype)
    for copy in sent:
        copy.wait_send()


def fused(n, queries, cache, cache_scale, offsets, lengths, clamp_code, w_out):
    tok_rows, head_dim = queries.shape
    local_len = cache.shape[1]
    rows = n // 4
    cols = w_out.shape[1] // n
    kv_shape = (2 * local_len + 16, head_dim)
    vmem = pl.BlockSpec(memory_space=pltpu.VMEM)
    hbm = pl.BlockSpec(memory_space=pltpu.HBM)
    bf16, f32 = jnp.bfloat16, jnp.float32
    dma = pltpu.SemaphoreType.DMA
    block = (tok_rows, cols)
    return pl.pallas_call(
        functools.partial(fused_kernel, n),
        out_shape=jax.ShapeDtypeStruct((cols, tok_rows), bf16),
        in_specs=[hbm] * 7,
        out_specs=vmem,
        scratch_shapes=[
            pltpu.VMEM(queries.shape, bf16),
            pltpu.VMEM(kv_shape, bf16),
            pltpu.VMEM(cache_scale.shape, bf16),
            pltpu.SMEM(offsets.shape, jnp.int32),
            pltpu.SMEM(lengths.shape, jnp.int32),
            pltpu.SMEM(clamp_code.shape, jnp.int32),
            pltpu.VMEM((rows, head_dim, cols), bf16),
            pltpu.VMEM((3, rows, head_dim, cols), bf16),
            pltpu.VMEM((n,) + kv_shape, bf16),
            pltpu.VMEM((n, tok_rows, local_len), f32),
            pltpu.VMEM((rows, tok_rows, head_dim), bf16),
            pltpu.VMEM((3, tok_rows, head_dim), f32),
            pltpu.VMEM((3, tok_rows, head_dim), f32),
            pltpu.VMEM((rows,) + block, bf16),
            pltpu.VMEM((rows,) + block, bf16),
            pltpu.VMEM((rows,) + block, bf16),
            pltpu.VMEM((rows,) + block, bf16),
            dma((7,)),
            dma((2 * rows,)),
            dma((3, rows)),
            dma((3, rows)),
            dma((3, rows)),
            dma((3, rows)),
            dma((rows,)),
            dma((rows,)),
            dma((2 * rows,)),
            dma((n,)),
            dma((rows,)),
            dma((rows,)),
            dma((2,)),
            dma((2,)),
            dma((rows,)),
            dma((rows,)),
            dma((rows,)),
            dma((rows,)),
        ],
        compiler_params=pltpu.CompilerParams(
            collective_id=0, has_side_effects=True, vmem_limit_bytes=40 * 1024 * 1024
        ),
        cost_estimate=pl.CostEstimate(
            flops=2 * tok_rows * head_dim * (2 * n * local_len + w_out.shape[1]),
            bytes_accessed=2 * w_out.size + 2 * cols * tok_rows,
            transcendentals=tok_rows * n * local_len,
        ),
    )(queries, cache, cache_scale, offsets, lengths, clamp_code, w_out)


def fits_fused(groups, n, queries, cache, w_out):
    head_dim, local_len = queries.shape[1], cache.shape[1]
    return (
        groups == 2
        and cache.shape[2] == head_dim
        and head_dim % 32 == 0
        and n % 4 == 0
        and n >= 16
        and (n & (n - 1)) == 0
        and local_len % head_dim == 0
        and 2 * local_len // head_dim <= 16
        and w_out.shape[1] % (n * 128) == 0
        and n * local_len <= 16384
    )


def per_device(groups, n, queries, cache, cache_scale, offsets, lengths, clamp_code, w_out):
    if fits_fused(groups, n, queries, cache, w_out):
        return fused(n, queries, cache, cache_scale, offsets, lengths, clamp_code, w_out)
    my_index = lax.axis_index("head")
    head_dim = queries.shape[1]
    local_len = cache.shape[1]
    kv_count = cache.shape[2] // head_dim
    gathered = lax.all_gather(queries, "head", axis=1, tiled=True)
    tok_rows = gathered.shape[0]
    head_count = gathered.shape[1] // head_dim
    per_group = head_count // kv_count
    token_ids = jnp.arange(tok_rows, dtype=jnp.int32)
    request = token_ids // SPAN
    within = token_ids % SPAN
    req_match = request[:, None] == jnp.arange(offsets.shape[0], dtype=jnp.int32)[None, :]
    starts = jnp.sum(jnp.where(req_match, offsets[None, :], 0), axis=1)
    last_pos = starts + jnp.sum(jnp.where(req_match, lengths[None, :], 0), axis=1) - SPAN + within
    inv_root = 1.0 / math.sqrt(head_dim)
    positions = my_index * local_len + jnp.arange(local_len, dtype=jnp.int32)
    visible = (positions[None, :] >= starts[:, None]) & (positions[None, :] <= last_pos[:, None])
    max_parts = []
    for kv_index in range(kv_count):
        column_left = kv_index * head_dim
        query_block = gathered[
            :, column_left * per_group : (column_left + head_dim) * per_group
        ].reshape(tok_rows, per_group, head_dim)
        masked = masked_scores(
            query_block,
            cache[0, :, column_left : column_left + head_dim],
            cache_scale[0, kv_index],
            visible,
            inv_root,
        )
        max_parts.append(jnp.max(masked, axis=2))
    local_max = jnp.concatenate(max_parts, 0)
    global_max = lax.pmax(local_max, "head")
    numer_parts = []
    denom_parts = []
    for kv_index in range(kv_count):
        column_left = kv_index * head_dim
        query_block = gathered[
            :, column_left * per_group : (column_left + head_dim) * per_group
        ].reshape(tok_rows, per_group, head_dim)
        masked = masked_scores(
            query_block,
            cache[0, :, column_left : column_left + head_dim],
            cache_scale[0, kv_index],
            visible,
            inv_root,
        )
        row_max = global_max[kv_index * per_group : (kv_index + 1) * per_group]
        numer_part, denom_part = tile_sums(
            masked,
            row_max,
            visible,
            cache_scale[1, kv_index],
            cache[1, :, column_left : column_left + head_dim],
        )
        numer_parts.append(numer_part)
        denom_parts.append(denom_part)
    numerator = jnp.concatenate(numer_parts, 0)
    denominator = jnp.concatenate(denom_parts, 0)
    numer_rows, denom_rows = (
        lax.psum_scatter(numerator, "head", scatter_dimension=1, tiled=True),
        lax.psum_scatter(denominator, "head", scatter_dimension=1, tiled=True),
    )
    token_attention = (numer_rows / denom_rows[..., None]).astype(jnp.bfloat16)
    clip_limit = clamp_code[0].astype(jnp.float32) / 1024.0
    scale_out = 1.0 / math.sqrt(head_count * head_dim)
    hd_matrix = hadamard(head_dim).astype(jnp.bfloat16)
    inner_mixed = jnp.einsum(
        "hrd,de->hre", token_attention, hd_matrix, preferred_element_type=jnp.float32
    )
    rotated = jnp.einsum(
        "gh,hre->gre", hadamard(head_count), inner_mixed, precision=lax.Precision.HIGHEST
    )
    clamped = jnp.clip(rotated * scale_out, -clip_limit, clip_limit).astype(jnp.bfloat16)
    activation = lax.all_to_all(clamped, "head", split_axis=0, concat_axis=1, tiled=True)[0]
    projected = lax.psum_scatter(
        lax.dot_general(
            w_out, activation, (((0,), (1,)), ((), ())), preferred_element_type=jnp.float32
        ),
        "head",
        scatter_dimension=0,
        tiled=True,
    )
    return projected.astype(jnp.bfloat16)


def solution(mesh):
    return jax.shard_map(
        functools.partial(per_device, mesh.shape["groups"], mesh.shape["head"]),
        mesh=mesh,
        in_specs=(
            P("groups", "head"),
            P(None, ("groups", "head"), None),
            P(None, None, ("groups", "head")),
            P("groups"),
            P("groups"),
            P("groups"),
            P("head", None),
        ),
        out_specs=P("head", "groups"),
        check_vma=False,
    )
```

```python
import functools
import math

import jax
import jax.numpy as jnp
from jax import lax
from jax.experimental import pallas as pl
from jax.experimental.pallas import tpu as pltpu
from jax.sharding import PartitionSpec as P

SPAN = 64


NEG_FILL = -1e30

EARLY = 1

LATE = 2


def hadamard(matrix_size):
    counter_index = jnp.arange(matrix_size, dtype=jnp.int32)
    common = counter_index[:, None] & counter_index[None, :]
    parity = jnp.zeros((matrix_size, matrix_size), jnp.int32)
    for bit_place in range(matrix_size.bit_length() - 1):
        parity = parity + (common >> bit_place & 1)
    return jnp.where(parity % 2 == 0, 1.0, -1.0).astype(jnp.float32)


def masked_scores(query_block, key_rows, key_scale, visible_tile, inv_root):
    scores = jnp.einsum("tjd,pd->jtp", query_block, key_rows, preferred_element_type=jnp.float32)
    scores = scores * (key_scale.astype(jnp.float32) * inv_root)[None, None, :]
    return jnp.where(visible_tile[None], scores, NEG_FILL)


def tile_sums(masked, row_max, visible_tile, value_scale, value_rows):
    weights = jnp.where(visible_tile[None], jnp.exp(masked - row_max[..., None]), 0.0)
    prob_rows = (weights * value_scale.astype(jnp.float32)[None, None, :]).astype(jnp.bfloat16)
    numerator = jnp.einsum("jtp,pd->jtd", prob_rows, value_rows, preferred_element_type=jnp.float32)
    return (numerator, jnp.sum(weights, axis=2))


def fused_kernel(
    n,
    queries_hbm,
    cache_hbm,
    scale_hbm,
    offsets_hbm,
    lengths_hbm,
    clamp_hbm,
    w_out,
    out,
    queries,
    kv_own,
    scale_own,
    offsets,
    lengths,
    clamp_code,
    w_own,
    w_quad,
    kv_all,
    scores,
    att_all,
    mix_send,
    mix_recv,
    z_send,
    z_recv,
    y_send,
    y_recv,
    own_sem,
    w_sem,
    wq_ssem,
    wq_rsem,
    wx_ssem,
    wx_rsem,
    kv_zsem,
    kv_ysem,
    kv_csem,
    kv_rsem,
    att_ssem,
    att_rsem,
    mix_ssem,
    mix_rsem,
    z_ssem,
    z_rsem,
    y_ssem,
    y_rsem,
):
    f32, bf16 = jnp.float32, jnp.bfloat16
    rows = n // 4
    tok_rows, head_dim = queries.shape
    half_dim = head_dim // 2
    local_len = (kv_own.shape[0] - 16) // 2
    scale_rows = local_len // head_dim
    cols = out.shape[0]
    me = lax.axis_index("head")
    group = lax.axis_index("groups")
    z, y, c = lax.div(me, 4), lax.rem(lax.div(me, 2), 2), lax.rem(me, 2)

    def place(zz, yy, cc):
        return zz * 4 + yy * 2 + cc

    def z_at(step):
        return lax.rem(z + step, rows)

    y_peer, c_peer = place(z, 1 - y, c), place(z, y, 1 - c)
    quad = (place(z, y, c), c_peer, y_peer, place(z, 1 - y, 1 - c))
    peers = [place(z_at(d), y, c) for d in range(1, rows)] + list(quad[1:])

    locals_in = (
        (cache_hbm.at[0], kv_own.at[pl.ds(0, local_len)]),
        (cache_hbm.at[1], kv_own.at[pl.ds(local_len, local_len)]),
        (scale_hbm, scale_own),
        (queries_hbm, queries),
        (offsets_hbm, offsets),
        (lengths_hbm, lengths),
        (clamp_hbm, clamp_code),
    )
    own_copies = [
        pltpu.make_async_copy(src, dst, own_sem.at[i]) for i, (src, dst) in enumerate(locals_in)
    ]
    for copy in own_copies:
        copy.start()

    def remote(src, dst, ssem, rsem, peer, to_group=None):
        target = {"head": peer}
        if to_group is not None:
            target["groups"] = to_group
        return pltpu.make_async_remote_copy(
            src_ref=src,
            dst_ref=dst,
            send_sem=ssem,
            recv_sem=rsem,
            device_id=target,
            device_id_type=pl.DeviceIdType.MESH,
        )

    barrier = pltpu.get_barrier_semaphore()
    for peer in peers:
        pl.semaphore_signal(
            barrier, inc=1, device_id={"head": peer}, device_id_type=pl.DeviceIdType.MESH
        )
    pl.semaphore_signal(
        barrier,
        inc=1,
        device_id={"head": me, "groups": 1 - group},
        device_id_type=pl.DeviceIdType.MESH,
    )
    for copy in own_copies[:3]:
        copy.wait()
    scale_lines = scale_own[...].astype(f32)
    lines = [
        scale_lines[which, :, i * head_dim : (i + 1) * head_dim]
        for which in range(2)
        for i in range(scale_rows)
    ]
    lines.append(jnp.zeros((16 - len(lines), head_dim), f32))
    kv_own[2 * local_len : 2 * local_len + 16, :] = jnp.concatenate(lines, axis=0).astype(bf16)
    pl.semaphore_wait(barrier, len(peers) + 1)

    sent = []

    def send(*args):
        copy = remote(*args)
        copy.start()
        sent.append(copy)

    kv_steps = [d for d in range(1, rows) if 2 * d != rows]
    for d in kv_steps:
        send(kv_own, kv_all.at[me], kv_zsem.at[d], kv_rsem.at[me], place(z_at(d), y, c))
    first_sends = list(sent)
    send(kv_own, kv_all.at[me], kv_ysem.at[0], kv_rsem.at[me], y_peer)
    send(kv_own, kv_all.at[me], kv_csem.at[0], kv_rsem.at[me], c_peer)

    def w_columns(d, yy, cc):
        row = z_at(d - d % 2)
        row = row + (1 - 2 * lax.rem(row, 2)) * (d % 2)
        return pl.ds(pl.multiple_of(place(row, yy, cc) * cols, cols), cols)

    quad_at = ((y, c), (y, 1 - c), (1 - y, c), (1 - y, 1 - c))
    my_half = pl.ds(pl.multiple_of(group * half_dim, half_dim), half_dim)

    other_half = pl.ds(pl.multiple_of((1 - group) * half_dim, half_dim), half_dim)

    def w_share(d):
        for k in (2, 3):
            send(
                w_out.at[my_half, w_columns(d, *quad_at[k])],
                w_quad.at[k - 1, d, my_half],
                wq_ssem.at[k - 1, d],
                wq_rsem.at[k - 1, d],
                quad[k],
            )

    def w_core(d):
        send(
            w_out.at[:, w_columns(d, *quad_at[1])],
            w_quad.at[0, d],
            wq_ssem.at[0, d],
            wq_rsem.at[0, d],
            quad[1],
        )

    def w_forward(d):
        for k in (1, 2):
            mine = w_quad.at[k, d, my_half]
            remote(mine, mine, wq_ssem.at[k, d], wq_rsem.at[k, d], y_peer).wait_recv()
            send(mine, mine, wx_ssem.at[k, d], wx_rsem.at[k, d], me, 1 - group)

    def w_wait(d):
        full = w_quad.at[0, d]
        remote(full, full, wq_ssem.at[0, d], wq_rsem.at[0, d], y_peer).wait_recv()
        for k in (1, 2) if d in shared else ():
            half = w_quad.at[k, d, other_half]
            remote(half, half, wx_ssem.at[k, d], wx_rsem.at[k, d], me, 1 - group).wait_recv()

    steps = [d for p in range(1, rows // 2) for d in (2 * p + 1, 2 * p)] + [1, 0]
    late = steps[len(steps) - LATE :]
    shared = steps[: len(steps) - LATE]
    w_copies = [
        pltpu.make_async_copy(w_out.at[:, w_columns(d, y, c)], w_own.at[d], w_sem.at[d])
        for d in range(rows)
    ]
    late_copies = {
        d: pltpu.make_async_copy(
            w_out.at[:, w_columns(d, 1 - y, c)], w_quad.at[1, d], w_sem.at[rows + d]
        )
        for d in late
    }
    for copy in w_copies + list(late_copies.values()):
        copy.start()
    for d in shared[:EARLY]:
        w_share(d)
    for d in steps:
        w_core(d)
    for d in late:
        send(
            w_out.at[:, w_columns(d, 1 - y, 1 - c)],
            w_quad.at[2, d],
            wq_ssem.at[2, d],
            wq_rsem.at[2, d],
            c_peer,
        )

    def kv_wait(slot):
        remote(kv_all.at[slot], kv_all.at[slot], kv_zsem.at[0], kv_rsem.at[slot], c_peer).wait_recv()

    for copy in own_copies[3:]:
        copy.wait()
    token = lax.broadcasted_iota(jnp.int32, (tok_rows, 1), 0)
    starts = jnp.zeros((tok_rows, 1), jnp.int32)
    ends = jnp.zeros((tok_rows, 1), jnp.int32)
    for r in range(tok_rows // SPAN):
        mine = (token >= r * SPAN) & (token < (r + 1) * SPAN)
        starts = jnp.where(mine, offsets[r], starts)
        ends = jnp.where(mine, offsets[r] + lengths[r] - SPAN + token - r * SPAN, ends)
    inv_root = 1.0 / math.sqrt(head_dim)
    lane = lax.broadcasted_iota(jnp.int32, (tok_rows, local_len), 1)

    def scale_line(block, which):
        first = 2 * local_len + which * scale_rows
        lines = block[2 * local_len : 2 * local_len + 16, :].astype(f32)
        at = first - 2 * local_len
        return jnp.concatenate([lines[at + i : at + i + 1, :] for i in range(scale_rows)], axis=1)

    order = []
    maxima = []

    def score_block(slot, block):
        keys = block[0:local_len, :]
        part = lax.dot_general(
            queries[...], keys, (((1,), (1,)), ((), ())), preferred_element_type=f32
        )
        part = part * (scale_line(block, 0) * inv_root)
        positions = slot * local_len + lane
        part = jnp.where((positions >= starts) & (positions <= ends), part, NEG_FILL)
        scores[len(order)] = part
        order.append(block)
        maxima.append(jnp.max(part, axis=1, keepdims=True))

    score_block(me, kv_own)
    for copy in first_sends:
        copy.wait_send()
        sent.remove(copy)
    d = rows // 2
    kv_steps.append(d)
    send(kv_own, kv_all.at[me], kv_zsem.at[d], kv_rsem.at[me], place(z_at(d), y, c))
    for d in kv_steps:
        slot = place(z_at(d), y, c)
        kv_wait(slot)
        send(kv_all.at[slot], kv_all.at[slot], kv_ysem.at[d], kv_rsem.at[slot], y_peer)
        send(kv_all.at[slot], kv_all.at[slot], kv_csem.at[d], kv_rsem.at[slot], c_peer)
        score_block(slot, kv_all.at[slot])
    for d in range(rows):
        slot = place(z_at(d), 1 - y, c)
        kv_wait(slot)
        send(kv_all.at[slot], kv_all.at[slot], kv_csem.at[rows + d], kv_rsem.at[slot], c_peer)
        score_block(slot, kv_all.at[slot])
    for d in shared[EARLY:]:
        w_share(d)
    for d in shared[:EARLY]:
        w_forward(d)
    for yy in (y, 1 - y):
        for d in range(rows):
            slot = place(z_at(d), yy, 1 - c)
            kv_wait(slot)
            score_block(slot, kv_all.at[slot])

    row_max = functools.reduce(jnp.maximum, maxima)
    numerator = jnp.zeros((tok_rows, head_dim), f32)
    denominator = jnp.zeros((tok_rows, 1), f32)
    for step, block in enumerate(order):
        weights = jnp.exp(scores[step] - row_max)
        denominator = denominator + jnp.sum(weights, axis=1, keepdims=True)
        probs = (weights * scale_line(block, 1)).astype(bf16)
        numerator = numerator + jnp.dot(
            probs, block[local_len : 2 * local_len, :], preferred_element_type=f32
        )
    att_all[z] = (numerator / denominator).astype(bf16)

    for d in range(1, rows):
        send(att_all.at[z], att_all.at[z], att_ssem.at[d], att_rsem.at[z], place(z_at(d), y, c))
    for d in shared[EARLY:3]:
        w_forward(d)
    down = lax.broadcasted_iota(jnp.int32, (head_dim, head_dim), 0)
    across = lax.broadcasted_iota(jnp.int32, (head_dim, head_dim), 1)
    common = down & across
    parity = jnp.zeros((head_dim, head_dim), jnp.int32)
    for bit in range(head_dim.bit_length() - 1):
        parity = parity + ((common >> bit) & 1)
    hd_matrix = jnp.where((parity & 1) == 0, 1.0, -1.0).astype(f32)
    for d in range(1, rows):
        zz = z_at(d)
        remote(att_all.at[zz], att_all.at[zz], att_ssem.at[0], att_rsem.at[zz], y_peer).wait_recv()
    mixed = jnp.zeros((tok_rows, head_dim), f32)
    for zz in range(rows):
        odd = 0
        for bit in range(rows.bit_length() - 1):
            if zz >> bit & 1:
                odd = odd + lax.rem(lax.div(z, 1 << bit), 2)
        sign = (1 - 2 * lax.rem(odd, 2)).astype(f32) if zz else 1.0
        mixed = mixed + att_all[zz].astype(f32) * sign
    mixed = jnp.dot(mixed, hd_matrix, precision=lax.Precision.HIGHEST, preferred_element_type=f32)

    def swap(at, size, level, peer):
        there = remote(
            mix_send.at[pl.ds(at, size)],
            mix_recv.at[pl.ds(at, size)],
            mix_ssem.at[level],
            mix_rsem.at[level],
            peer,
        )
        there.start()
        sent.append(there)
        return there

    mix_send[0] = mixed
    there = swap(0, 1, 0, y_peer)
    for d in shared[max(EARLY, 3):]:
        w_forward(d)
    there.wait_recv()
    y_sign, c_sign = (1 - 2 * y).astype(f32), (1 - 2 * c).astype(f32)
    pair = (mixed * y_sign + mix_recv[0], mixed - mix_recv[0] * y_sign)
    mix_send[1] = pair[0]
    mix_send[2] = pair[1]
    there = swap(1, 2, 1, c_peer)
    there.wait_recv()
    limit = clamp_code[0].astype(f32) / 1024.0
    scale_out = 1.0 / math.sqrt(n * head_dim)
    acts = []
    for i in range(2):
        for full in (pair[i] * c_sign + mix_recv[1 + i], pair[i] - mix_recv[1 + i] * c_sign):
            acts.append(jnp.clip(full * scale_out, -limit, limit).astype(bf16))

    def row_sum(d):
        w_copies[d].wait()
        w_wait(d)
        total = jnp.dot(acts[0], w_own[d], preferred_element_type=f32)
        if d in late:
            total = total + jnp.dot(acts[1], w_quad[0, d], preferred_element_type=f32)
            remote(y_send.at[d], y_recv.at[d], y_ssem.at[d], y_rsem.at[d], y_peer).wait_recv()
            return total + y_recv[d].astype(f32)
        for k in range(3):
            total = total + jnp.dot(acts[k + 1], w_quad[k, d], preferred_element_type=f32)
        return total

    def z_wait(slot, peer):
        remote(
            z_send.at[slot], z_recv.at[slot], z_ssem.at[slot], z_rsem.at[slot], peer
        ).wait_recv()
        return z_recv[slot].astype(f32)

    def z_go(slot, value, peer):
        z_send[slot] = value.astype(bf16)
        send(z_send.at[slot], z_recv.at[slot], z_ssem.at[slot], z_rsem.at[slot], peer)

    far = rows // 2 - 1
    low = lax.rem(z, 2)
    z_mate = place(z + 1 - 2 * low, y, c)
    for p in range(1, far + 1):
        z_go(p - 1, row_sum(2 * p + 1), z_mate)
    for d in late:
        late_copies[d].wait()
        full = w_quad.at[2, d]
        remote(full, full, wq_ssem.at[2, d], wq_rsem.at[2, d], c_peer).wait_recv()
        theirs = jnp.dot(acts[0], w_quad[1, d], preferred_element_type=f32)
        theirs = theirs + jnp.dot(acts[1], w_quad[2, d], preferred_element_type=f32)
        y_send[d] = theirs.astype(bf16)
        send(y_send.at[d], y_recv.at[d], y_ssem.at[d], y_rsem.at[d], y_peer)
    kept = [row_sum(2 * p) for p in range(1, far + 1)]
    near = row_sum(1)
    for p in range(1, far + 1):
        peer = place(z_at(2 * p), y, c)
        z_go(far + p - 1, kept[p - 1] + z_wait(p - 1, z_mate), peer)
    z_go(2 * far, near, z_mate)
    total = row_sum(0)
    total = total + z_wait(2 * far, z_mate)
    for p in range(1, far + 1):
        total = total + z_wait(far + p - 1, z_mate)
    out[...] = total.T.astype(out.dtype)
    for copy in sent:
        copy.wait_send()


def fused(n, queries, cache, cache_scale, offsets, lengths, clamp_code, w_out):
    tok_rows, head_dim = queries.shape
    local_len = cache.shape[1]
    rows = n // 4
    cols = w_out.shape[1] // n
    kv_shape = (2 * local_len + 16, head_dim)
    vmem = pl.BlockSpec(memory_space=pltpu.VMEM)
    hbm = pl.BlockSpec(memory_space=pltpu.HBM)
    bf16, f32 = jnp.bfloat16, jnp.float32
    dma = pltpu.SemaphoreType.DMA
    block = (tok_rows, cols)
    return pl.pallas_call(
        functools.partial(fused_kernel, n),
        out_shape=jax.ShapeDtypeStruct((cols, tok_rows), bf16),
        in_specs=[hbm] * 7,
        out_specs=vmem,
        scratch_shapes=[
            pltpu.VMEM(queries.shape, bf16),
            pltpu.VMEM(kv_shape, bf16),
            pltpu.VMEM(cache_scale.shape, bf16),
            pltpu.SMEM(offsets.shape, jnp.int32),
            pltpu.SMEM(lengths.shape, jnp.int32),
            pltpu.SMEM(clamp_code.shape, jnp.int32),
            pltpu.VMEM((rows, head_dim, cols), bf16),
            pltpu.VMEM((3, rows, head_dim, cols), bf16),
            pltpu.VMEM((n,) + kv_shape, bf16),
            pltpu.VMEM((n, tok_rows, local_len), f32),
            pltpu.VMEM((rows, tok_rows, head_dim), bf16),
            pltpu.VMEM((3, tok_rows, head_dim), f32),
            pltpu.VMEM((3, tok_rows, head_dim), f32),
            pltpu.VMEM((rows,) + block, bf16),
            pltpu.VMEM((rows,) + block, bf16),
            pltpu.VMEM((rows,) + block, bf16),
            pltpu.VMEM((rows,) + block, bf16),
            dma((7,)),
            dma((2 * rows,)),
            dma((3, rows)),
            dma((3, rows)),
            dma((3, rows)),
            dma((3, rows)),
            dma((rows,)),
            dma((rows,)),
            dma((2 * rows,)),
            dma((n,)),
            dma((rows,)),
            dma((rows,)),
            dma((2,)),
            dma((2,)),
            dma((rows,)),
            dma((rows,)),
            dma((rows,)),
            dma((rows,)),
        ],
        compiler_params=pltpu.CompilerParams(
            collective_id=0, has_side_effects=True, vmem_limit_bytes=40 * 1024 * 1024
        ),
        cost_estimate=pl.CostEstimate(
            flops=2 * tok_rows * head_dim * (2 * n * local_len + w_out.shape[1]),
            bytes_accessed=2 * w_out.size + 2 * cols * tok_rows,
            transcendentals=tok_rows * n * local_len,
        ),
    )(queries, cache, cache_scale, offsets, lengths, clamp_code, w_out)


def fits_fused(groups, n, queries, cache, w_out):
    head_dim, local_len = queries.shape[1], cache.shape[1]
    return (
        groups == 2
        and cache.shape[2] == head_dim
        and head_dim % 32 == 0
        and n % 4 == 0
        and n >= 16
        and (n & (n - 1)) == 0
        and local_len % head_dim == 0
        and 2 * local_len // head_dim <= 16
        and w_out.shape[1] % (n * 128) == 0
        and n * local_len <= 16384
    )


def per_device(groups, n, queries, cache, cache_scale, offsets, lengths, clamp_code, w_out):
    if fits_fused(groups, n, queries, cache, w_out):
        return fused(n, queries, cache, cache_scale, offsets, lengths, clamp_code, w_out)
    my_index = lax.axis_index("head")
    head_dim = queries.shape[1]
    local_len = cache.shape[1]
    kv_count = cache.shape[2] // head_dim
    gathered = lax.all_gather(queries, "head", axis=1, tiled=True)
    tok_rows = gathered.shape[0]
    head_count = gathered.shape[1] // head_dim
    per_group = head_count // kv_count
    token_ids = jnp.arange(tok_rows, dtype=jnp.int32)
    request = token_ids // SPAN
    within = token_ids % SPAN
    req_match = request[:, None] == jnp.arange(offsets.shape[0], dtype=jnp.int32)[None, :]
    starts = jnp.sum(jnp.where(req_match, offsets[None, :], 0), axis=1)
    last_pos = starts + jnp.sum(jnp.where(req_match, lengths[None, :], 0), axis=1) - SPAN + within
    inv_root = 1.0 / math.sqrt(head_dim)
    positions = my_index * local_len + jnp.arange(local_len, dtype=jnp.int32)
    visible = (positions[None, :] >= starts[:, None]) & (positions[None, :] <= last_pos[:, None])
    max_parts = []
    for kv_index in range(kv_count):
        column_left = kv_index * head_dim
        query_block = gathered[
            :, column_left * per_group : (column_left + head_dim) * per_group
        ].reshape(tok_rows, per_group, head_dim)
        masked = masked_scores(
            query_block,
            cache[0, :, column_left : column_left + head_dim],
            cache_scale[0, kv_index],
            visible,
            inv_root,
        )
        max_parts.append(jnp.max(masked, axis=2))
    local_max = jnp.concatenate(max_parts, 0)
    global_max = lax.pmax(local_max, "head")
    numer_parts = []
    denom_parts = []
    for kv_index in range(kv_count):
        column_left = kv_index * head_dim
        query_block = gathered[
            :, column_left * per_group : (column_left + head_dim) * per_group
        ].reshape(tok_rows, per_group, head_dim)
        masked = masked_scores(
            query_block,
            cache[0, :, column_left : column_left + head_dim],
            cache_scale[0, kv_index],
            visible,
            inv_root,
        )
        row_max = global_max[kv_index * per_group : (kv_index + 1) * per_group]
        numer_part, denom_part = tile_sums(
            masked,
            row_max,
            visible,
            cache_scale[1, kv_index],
            cache[1, :, column_left : column_left + head_dim],
        )
        numer_parts.append(numer_part)
        denom_parts.append(denom_part)
    numerator = jnp.concatenate(numer_parts, 0)
    denominator = jnp.concatenate(denom_parts, 0)
    numer_rows, denom_rows = (
        lax.psum_scatter(numerator, "head", scatter_dimension=1, tiled=True),
        lax.psum_scatter(denominator, "head", scatter_dimension=1, tiled=True),
    )
    token_attention = (numer_rows / denom_rows[..., None]).astype(jnp.bfloat16)
    clip_limit = clamp_code[0].astype(jnp.float32) / 1024.0
    scale_out = 1.0 / math.sqrt(head_count * head_dim)
    hd_matrix = hadamard(head_dim).astype(jnp.bfloat16)
    inner_mixed = jnp.einsum(
        "hrd,de->hre", token_attention, hd_matrix, preferred_element_type=jnp.float32
    )
    rotated = jnp.einsum(
        "gh,hre->gre", hadamard(head_count), inner_mixed, precision=lax.Precision.HIGHEST
    )
    clamped = jnp.clip(rotated * scale_out, -clip_limit, clip_limit).astype(jnp.bfloat16)
    activation = lax.all_to_all(clamped, "head", split_axis=0, concat_axis=1, tiled=True)[0]
    projected = lax.psum_scatter(
        lax.dot_general(
            w_out, activation, (((0,), (1,)), ((), ())), preferred_element_type=jnp.float32
        ),
        "head",
        scatter_dimension=0,
        tiled=True,
    )
    return projected.astype(jnp.bfloat16)


def solution(mesh):
    return jax.shard_map(
        functools.partial(per_device, mesh.shape["groups"], mesh.shape["head"]),
        mesh=mesh,
        in_specs=(
            P("groups", "head"),
            P(None, ("groups", "head"), None),
            P(None, None, ("groups", "head")),
            P("groups"),
            P("groups"),
            P("groups"),
            P("head", None),
        ),
        out_specs=P("head", "groups"),
        check_vma=False,
    )
```
